32 devices in a mesh: replica: 4 (over y, x), shard: 8 (over z, core).
Axes of the slice: x: 2, y: 2, z: 4, core: 2. Of those that a mesh axis runs over, the one named last changes fastest.
Arguments:
- inputs: bfloat16 [8192, 6144], P(('replica', 'shard')), may hold values from -6 to 6
- doc_ids: int32 [32, 256], P(('replica', 'shard')), may hold values from 0 to 7, never falling along the last dimension, each value on 1 to 64 neighbouring positions
- values: bfloat16 [8192, 128], P(('replica', 'shard')), may hold values from -6 to 6
- cotangent: bfloat16 [8192, 128], P(('replica', 'shard')), may hold values from -24 to 24
- weights: float32 [24576, 256], P(('replica', 'shard')), may hold values from -6 to 6
- moment1: float32 [24576, 256], P(('replica', 'shard')), may hold values from -3 to 3
- moment2: float32 [24576, 256], P(('replica', 'shard')), may hold values from 0.05 to 2
- frag_local: bfloat16 [4, 16, 8, 6144], P('replica', None, 'shard'), may hold values from -6 to 6
- frag_global: float32 [16, 8, 6144], P(None, 'shard'), may hold values from -6 to 6
- frag_moment: float32 [16, 8, 6144], P(None, 'shard'), may hold values from -3 to 3
- frag_index: int32 [1], replicated, may hold values from 0 to 15
Outputs:
- new_weights: float32 [24576, 256], P(('replica', 'shard'))
- new_moment1: float32 [24576, 256], P(('replica', 'shard'))
- new_moment2: float32 [24576, 256], P(('replica', 'shard'))
- new_global: float32 [8, 6144], P('shard')
- new_moment: float32 [8, 6144], P('shard')
The draws below stay inside these ranges and needn't reach their ends.
Inputs may be any that keep to these rules, and one draw needn't show every extreme that they name: `doc_ids`: within each row document numbers start at 0, never fall, and each document has 1 to 64 tokens; some document has exactly 64.
All inputs are finite; a program needn't handle non-finite values.
Results may differ from the reference program's by a relative error of at most 0.008.
Values may be sent and summed in bfloat16 or wider, within the bound.
No kernel may reach another device: no remote copies, remote signals or barrier semaphores. Data moves between devices by JAX's collectives and lax.ppermute only.
A program may use at most 64 MiB of HBM per device.

```python
import math
import jax
import jax.numpy as jnp
import numpy as np
from jax import lax

D = 6144
HEAD = 128
TOK_DEV = 256
FRAGS = 16
ADAM_STEP = 100
FRAG_ROWS = 8
TOKENS = 8192
SEQS = 32
N_REPLICA = 4
N_SHARD = 8


def block_levels(own_key, extent, cuts, least, high):
    def one(dim, parts):
        draws = jax.random.uniform(jax.random.fold_in(jax.random.fold_in(own_key, 6), dim), (parts,), jnp.float32, least / len(cuts), high / len(cuts))
        return jnp.repeat(jnp.exp(draws), extent[dim] // parts).reshape((-1,) + (1,) * (len(extent) - dim - 1))

    loudness = one(*cuts[0])
    for cut in cuts[1:]:
        loudness = loudness * one(*cut)
    return loudness


def profile(amount, total, most, slope):
    portions = [(1 << 20) // math.isqrt(rank ** slope) + 1 for rank in range(2, amount + 1)]
    rest, given = total - most - (amount - 1), [1] * (amount - 1)
    while rest > 0:
        free = [i for i in range(amount - 1) if given[i] < most]
        whole, budget = sum([portions[i] for i in free]), rest
        for i in free:
            more = min(most - given[i], max(1, budget * portions[i] // whole), rest)
            given[i] = given[i] + more
            rest = rest - more
    return np.array([most] + given)


def ragged_sizes(own_key, count, total, bound, lean):
    if count == 2:
        one = jax.random.randint(own_key, (), max(1, total - bound), min(bound, total - 1) + 1)
        return jnp.stack([one, total - one])
    tallies = jnp.asarray(profile(count, total, bound, lean), jnp.int32)
    couples = (count - 1) // 2
    source_of, taker = tallies[1:1 + 2 * couples:2], tallies[2:2 + 2 * couples:2]
    slack = jnp.minimum(source_of - 1, bound - taker)
    shifted = jax.random.randint(jax.random.fold_in(own_key, 1), (couples,), 0, 1 << 20) % (slack + 1)
    tallies = tallies.at[1:1 + 2 * couples:2].set(source_of - shifted).at[2:2 + 2 * couples:2].set(taker + shifted)
    return tallies[jax.random.permutation(jax.random.fold_in(own_key, 2), count)]


def bell_draw(own_key, dims, width, limit, split=(), kind=jnp.bfloat16):
    level = block_levels(own_key, dims, split, -0.22, 0.18) if split else 1.0
    values = jax.random.normal(own_key, dims, jnp.float32) * width * level
    return jnp.minimum(jnp.maximum(values, -limit), limit).astype(kind)


def setup_inputs(seed: int = 0) -> dict:
    keys = jax.random.split(jax.random.key(seed), 12)
    return {
        "inputs": bell_draw(keys[0], (TOKENS, D), 1.0, 6.0, ((0, 32),)),
        "doc_ids": jax.vmap(lambda own: jnp.searchsorted(jnp.cumsum(ragged_sizes(own, 8, TOK_DEV, TOK_DEV // 4, 1)), jnp.arange(TOK_DEV), side="right"))(jax.random.split(keys[1], SEQS)).reshape((SEQS, TOK_DEV)).astype(jnp.int32),
        "values": bell_draw(keys[2], (TOKENS, HEAD), 1.0, 6.0, ((0, 32),)),
        "cotangent": bell_draw(keys[3], (TOKENS, HEAD), 4.0, 24.0, ((0, 32),)),
        "weights": bell_draw(keys[4], (N_REPLICA * D, 2 * HEAD), 1.0, 6.0, ((0, 32),), jnp.float32),
        "moment1": bell_draw(keys[5], (N_REPLICA * D, 2 * HEAD), 0.5, 3.0, ((0, 32),), jnp.float32),
        "moment2": jnp.clip(jnp.exp(math.log(2.0) - 3.6888794 * jax.random.uniform(keys[6], (N_REPLICA * D, 2 * HEAD), jnp.float32) ** block_levels(keys[6], (N_REPLICA * D, 2 * HEAD), ((0, 32),), -0.2, 0.2)), 0.05, 2.0),
        "frag_local": bell_draw(keys[7], (N_REPLICA, FRAGS, FRAG_ROWS, D), 1.0, 6.0, ((0, 4), (2, 8))),
        "frag_global": bell_draw(keys[8], (FRAGS, FRAG_ROWS, D), 1.0, 6.0, ((1, 8),), jnp.float32),
        "frag_moment": bell_draw(keys[9], (FRAGS, FRAG_ROWS, D), 0.5, 3.0, ((1, 8),), jnp.float32),
        "frag_index": jax.random.randint(keys[10], (1,), 0, FRAGS).astype(jnp.int32),
    }


epsilon = 1e-06
beta_one = 0.9
beta_two = 0.95
learn_rate = 0.01
decay_rate = 0.1
outer_momentum = 0.9
outer_rate = 0.7

def head_grads(inputs, doc_ids, values, cotangent, projected):
    model_width = inputs.shape[1]
    head_size = values.shape[1]
    input_scale = 1.0 / math.sqrt(model_width)
    score_scale = 1.0 / math.sqrt(head_size)
    scaled = projected * input_scale
    queries = scaled[:, :head_size]
    keys_part = scaled[:, head_size:]
    q_rate = lax.rsqrt(lax.optimization_barrier(jnp.mean(queries * queries, axis=1, keepdims=True)) + epsilon)
    k_rate = lax.rsqrt(lax.optimization_barrier(jnp.mean(keys_part * keys_part, axis=1, keepdims=True)) + epsilon)
    q_unit = queries * q_rate
    k_unit = keys_part * k_rate
    scores = jnp.dot(q_unit, k_unit.T, precision=lax.Precision.HIGHEST) * score_scale
    position = jnp.arange(doc_ids.shape[0])
    allowed = (doc_ids[:, None] == doc_ids[None, :]) & (position[None, :] <= position[:, None])
    raised = jnp.where(allowed, jnp.exp(scores), jnp.float32(0.0))
    attention = raised / lax.optimization_barrier(jnp.sum(raised, axis=1, keepdims=True))
    grad_attention = jnp.dot(cotangent, values.T, preferred_element_type=jnp.float32)
    grad_scores = attention * (grad_attention - lax.optimization_barrier(jnp.sum(attention * grad_attention, axis=1, keepdims=True))) * score_scale
    grad_qunit = jnp.dot(grad_scores, k_unit, precision=lax.Precision.HIGHEST)
    grad_kunit = jnp.dot(grad_scores.T, q_unit, precision=lax.Precision.HIGHEST)
    grad_query = q_rate * (grad_qunit - q_unit * lax.optimization_barrier(jnp.mean(grad_qunit * q_unit, axis=1, keepdims=True)))
    grad_keys = k_rate * (grad_kunit - k_unit * lax.optimization_barrier(jnp.mean(grad_kunit * k_unit, axis=1, keepdims=True)))
    return (jnp.concatenate([grad_query, grad_keys], axis=1) * input_scale).astype(jnp.bfloat16)

def adam_update(weight_rows, first, second, gradient):
    first_new = beta_one * first + (1.0 - beta_one) * gradient
    second_new = beta_two * second + (1.0 - beta_two) * gradient * gradient
    first_hat = first_new / (1.0 - beta_one ** ADAM_STEP)
    second_hat = second_new / (1.0 - beta_two ** ADAM_STEP)
    weight_new = weight_rows - learn_rate * (first_hat / (jnp.sqrt(second_hat) + 1e-08) + decay_rate * weight_rows)
    return (weight_new, first_new, second_new)

def reference(inputs, doc_ids, values, cotangent, weights, moment1, moment2, frag_local, frag_global, frag_moment, frag_index):
    tok_all = inputs.reshape(N_REPLICA, N_SHARD, TOK_DEV, D)
    ids_all = doc_ids.reshape(N_REPLICA, N_SHARD, TOK_DEV)
    val_all = values.reshape(N_REPLICA, N_SHARD, TOK_DEV, HEAD)
    cot_all = cotangent.reshape(N_REPLICA, N_SHARD, TOK_DEV, HEAD)
    w_all = weights.reshape(N_REPLICA, D, 2 * HEAD)
    first_all = moment1.reshape(N_REPLICA, D, 2 * HEAD)
    second_all = moment2.reshape(N_REPLICA, D, 2 * HEAD)

    def replica_update(packed):
        tok_rep, ids_rep, val_rep, cot_rep, w_rep, first_rep, second_rep = packed
        lowered = w_rep.astype(jnp.bfloat16)

        def one_device(running, device):
            tok_dev, ids_dev, val_dev, cot_dev = device
            projected = jnp.dot(tok_dev, lowered, preferred_element_type=jnp.float32)
            grad_projected = head_grads(tok_dev, ids_dev, val_dev, cot_dev, projected)
            partial_term = lax.dot_general(tok_dev, grad_projected, (((0,), (0,)), ((), ())), preferred_element_type=jnp.float32)
            rounded = lax.optimization_barrier(partial_term.astype(jnp.bfloat16))
            return (running + rounded.astype(jnp.float32), None)
        start_sum = jnp.zeros((D, 2 * HEAD), jnp.float32)
        gradient, _ = lax.scan(one_device, start_sum, (tok_rep, ids_rep, val_rep, cot_rep))
        return adam_update(w_rep, first_rep, second_rep, gradient)
    new_w, new_first, new_second = lax.map(replica_update, (tok_all, ids_all, val_all, cot_all, w_all, first_all, second_all))
    new_weights = new_w.reshape(N_REPLICA * D, 2 * HEAD)
    new_moment1 = new_first.reshape(N_REPLICA * D, 2 * HEAD)
    new_moment2 = new_second.reshape(N_REPLICA * D, 2 * HEAD)
    chosen = frag_index[0].astype(jnp.int32)
    current = lax.dynamic_index_in_dim(frag_global, chosen, 0, keepdims=False)
    moment_now = lax.dynamic_index_in_dim(frag_moment, chosen, 0, keepdims=False)
    local_all = lax.dynamic_index_in_dim(frag_local, chosen, 1, keepdims=False)
    drift = lax.optimization_barrier((current[None] - local_all.astype(jnp.float32)).astype(jnp.bfloat16))
    drift_mean = lax.optimization_barrier(jnp.sum(drift.astype(jnp.float32), axis=0)) / N_REPLICA
    new_moment = outer_momentum * moment_now + drift_mean
    new_global = current - outer_rate * (drift_mean + outer_momentum * new_moment)
    return (new_weights, new_moment1, new_moment2, new_global, new_moment)
```

```python
import math

import jax
import jax.numpy as jnp
from jax import lax
from jax.sharding import PartitionSpec as P

ADAM_STEP = 100
CHUNKS = 2


epsilon = 1e-06
beta_one = 0.9
beta_two = 0.95
learn_rate = 0.01
decay_rate = 0.1
outer_momentum = 0.9
outer_rate = 0.7


def head_grads(inputs, doc_ids, values, cotangent, projected):
    model_width = inputs.shape[1]
    head_size = values.shape[1]
    input_scale = 1.0 / math.sqrt(model_width)
    score_scale = 1.0 / math.sqrt(head_size)
    scaled = projected * input_scale
    queries = scaled[:, :head_size]
    keys_part = scaled[:, head_size:]
    q_rate = lax.rsqrt(jnp.mean(queries * queries, axis=1, keepdims=True) + epsilon)
    k_rate = lax.rsqrt(jnp.mean(keys_part * keys_part, axis=1, keepdims=True) + epsilon)
    q_unit = queries * q_rate
    k_unit = keys_part * k_rate
    scores = jnp.dot(q_unit, k_unit.T, precision=lax.Precision.HIGHEST) * score_scale
    position = jnp.arange(doc_ids.shape[0])
    allowed = (doc_ids[:, None] == doc_ids[None, :]) & (position[None, :] <= position[:, None])
    raised = jnp.where(allowed, jnp.exp(scores), jnp.float32(0.0))
    attention = raised / jnp.sum(raised, axis=1, keepdims=True)
    grad_attention = jnp.dot(cotangent, values.T, preferred_element_type=jnp.float32)
    grad_scores = (
        attention
        * (grad_attention - jnp.sum(attention * grad_attention, axis=1, keepdims=True))
        * score_scale
    )
    grad_qunit = jnp.dot(grad_scores, k_unit, precision=lax.Precision.HIGHEST)
    grad_kunit = jnp.dot(grad_scores.T, q_unit, precision=lax.Precision.HIGHEST)
    grad_query = q_rate * (
        grad_qunit - q_unit * jnp.mean(grad_qunit * q_unit, axis=1, keepdims=True)
    )
    grad_keys = k_rate * (
        grad_kunit - k_unit * jnp.mean(grad_kunit * k_unit, axis=1, keepdims=True)
    )
    return (jnp.concatenate([grad_query, grad_keys], axis=1) * input_scale).astype(jnp.bfloat16)


def inner_step(inputs, doc_ids, values, cotangent, weights, moment1, moment2):
    devices = lax.axis_size("shard")
    chips = devices // 2
    here = lax.axis_index("shard")
    core = here % 2
    rows = weights.shape[0]
    part = rows // CHUNKS
    ring = [(i, (i + 2) % devices) for i in range(devices)]
    swap = [(i, i ^ 1) for i in range(devices)]

    def ordered(which):
        return [
            lax.dynamic_slice_in_dim(
                inputs, ((here - core - 2 * k) % devices + which) * rows, rows, axis=1
            )
            for k in range(chips)
        ]

    blocks = [weights[j * part : (j + 1) * part].astype(jnp.bfloat16) for j in range(CHUNKS)]
    flying = [lax.ppermute(block, "shard", ring) for block in blocks]
    mine = ordered(core)
    theirs = lax.ppermute(jnp.stack(ordered(1 - core)), "shard", swap)
    both = [jnp.concatenate([mine[k], theirs[k]], axis=0) for k in range(chips)]
    total = jnp.float32(0.0)
    for k in range(chips):
        for j in range(CHUNKS):
            total = total + jnp.dot(
                both[k][:, j * part : (j + 1) * part],
                blocks[j],
                preferred_element_type=jnp.float32,
            )
        if k < chips - 1:
            blocks = flying
            if k < chips - 2:
                flying = [lax.ppermute(block, "shard", ring) for block in blocks]
    tokens = inputs.shape[0]
    projected = total[:tokens] + lax.ppermute(total[tokens:], "shard", swap)
    grad_own = head_grads(inputs, doc_ids[0], values, cotangent, projected)
    grad_both = jnp.concatenate([grad_own, lax.ppermute(grad_own, "shard", swap)], axis=0)

    def term(k, j):
        return lax.dot_general(
            both[k][:, j * part : (j + 1) * part],
            grad_both,
            (((0,), (0,)), ((), ())),
            preferred_element_type=jnp.float32,
        )

    sums = [term(1, j).astype(jnp.bfloat16) for j in range(CHUNKS)]
    for k in range(chips - 1):
        later = 0 if k == chips - 2 else k + 2
        for j in range(CHUNKS):
            sums[j] = lax.ppermute(sums[j], "shard", ring).astype(jnp.float32) + term(later, j)
            if later:
                sums[j] = sums[j].astype(jnp.bfloat16)
    gradient = jnp.concatenate(sums, axis=0)
    first_new = beta_one * moment1 + (1.0 - beta_one) * gradient
    second_new = beta_two * moment2 + (1.0 - beta_two) * gradient * gradient
    first_hat = first_new / (1.0 - beta_one**ADAM_STEP)
    second_hat = second_new / (1.0 - beta_two**ADAM_STEP)
    weight_new = weights - learn_rate * (
        first_hat / (jnp.sqrt(second_hat) + 1e-08) + decay_rate * weights
    )
    return (weight_new, first_new, second_new)


def outer_step(frag_local, frag_global, frag_moment, frag_index):
    chosen = frag_index[0]
    current = lax.dynamic_index_in_dim(frag_global, chosen, 0, keepdims=False)
    moment_now = lax.dynamic_index_in_dim(frag_moment, chosen, 0, keepdims=False)
    local_copy = lax.dynamic_index_in_dim(frag_local[0], chosen, 0, keepdims=False)
    lowered_drift = lax.optimization_barrier(
        (current - local_copy.astype(jnp.float32)).astype(jnp.bfloat16)
    )
    drift = lowered_drift.astype(jnp.float32)
    replicas = lax.axis_size("replica")
    total = drift
    step = 1
    while step < replicas:
        total = total + lax.ppermute(total, "replica", [(i, i ^ step) for i in range(replicas)])
        step = 2 * step
    drift_mean = total / replicas
    new_moment = outer_momentum * moment_now + drift_mean
    new_global = current - outer_rate * (drift_mean + outer_momentum * new_moment)
    return (new_global, new_moment)


def on_device(
    inputs,
    doc_ids,
    values,
    cotangent,
    weights,
    moment1,
    moment2,
    frag_local,
    frag_global,
    frag_moment,
    frag_index,
):
    new_weights, new_moment1, new_moment2 = inner_step(
        inputs, doc_ids, values, cotangent, weights, moment1, moment2
    )
    new_global, new_moment = outer_step(frag_local, frag_global, frag_moment, frag_index)
    return (new_weights, new_moment1, new_moment2, new_global, new_moment)


def solution(mesh):
    placed = (
        P(("replica", "shard"), None),
        P(("replica", "shard"), None),
        P(("replica", "shard"), None),
        P(("replica", "shard"), None),
        P(("replica", "shard"), None),
        P(("replica", "shard"), None),
        P(("replica", "shard"), None),
        P("replica", None, "shard", None),
        P(None, "shard", None),
        P(None, "shard", None),
        P(),
    )
    return jax.shard_map(
        on_device,
        mesh=mesh,
        in_specs=placed,
        out_specs=(
            P(("replica", "shard"), None),
            P(("replica", "shard"), None),
            P(("replica", "shard"), None),
            P("shard", None),
            P("shard", None),
        ),
        check_vma=False,
    )
```

```python
import math

import jax
import jax.numpy as jnp
from jax import lax
from jax.sharding import PartitionSpec as P

ADAM_STEP = 100
CHUNKS = 3


epsilon = 1e-06
beta_one = 0.9
beta_two = 0.95
learn_rate = 0.01
decay_rate = 0.1
outer_momentum = 0.9
outer_rate = 0.7


def head_grads(inputs, doc_ids, values, cotangent, projected):
    model_width = inputs.shape[1]
    head_size = values.shape[1]
    input_scale = 1.0 / math.sqrt(model_width)
    score_scale = 1.0 / math.sqrt(head_size)
    scaled = projected * input_scale
    queries = scaled[:, :head_size]
    keys_part = scaled[:, head_size:]
    q_rate = lax.rsqrt(jnp.mean(queries * queries, axis=1, keepdims=True) + epsilon)
    k_rate = lax.rsqrt(jnp.mean(keys_part * keys_part, axis=1, keepdims=True) + epsilon)
    q_unit = queries * q_rate
    k_unit = keys_part * k_rate
    scores = jnp.dot(q_unit, k_unit.T, precision=lax.Precision.HIGHEST) * score_scale
    position = jnp.arange(doc_ids.shape[0])
    allowed = (doc_ids[:, None] == doc_ids[None, :]) & (position[None, :] <= position[:, None])
    raised = jnp.where(allowed, jnp.exp(scores), jnp.float32(0.0))
    attention = raised / jnp.sum(raised, axis=1, keepdims=True)
    grad_attention = jnp.dot(cotangent, values.T, preferred_element_type=jnp.float32)
    grad_scores = (
        attention
        * (grad_attention - jnp.sum(attention * grad_attention, axis=1, keepdims=True))
        * score_scale
    )
    grad_qunit = jnp.dot(grad_scores, k_unit, precision=lax.Precision.HIGHEST)
    grad_kunit = jnp.dot(grad_scores.T, q_unit, precision=lax.Precision.HIGHEST)
    grad_query = q_rate * (
        grad_qunit - q_unit * jnp.mean(grad_qunit * q_unit, axis=1, keepdims=True)
    )
    grad_keys = k_rate * (
        grad_kunit - k_unit * jnp.mean(grad_kunit * k_unit, axis=1, keepdims=True)
    )
    return (jnp.concatenate([grad_query, grad_keys], axis=1) * input_scale).astype(jnp.bfloat16)


def outer_start(frag_local, frag_global, frag_moment, frag_index):
    chosen = frag_index[0]
    current = lax.dynamic_index_in_dim(frag_global, chosen, 0, keepdims=False)
    moment_now = lax.dynamic_index_in_dim(frag_moment, chosen, 0, keepdims=False)
    local_copy = lax.dynamic_index_in_dim(frag_local[0], chosen, 0, keepdims=False)
    drift = (current - local_copy.astype(jnp.float32)).astype(jnp.bfloat16)
    return current, moment_now, lax.optimization_barrier(drift).astype(jnp.float32)


def exchange(total, step):
    replicas = lax.axis_size("replica")
    return total + lax.ppermute(total, "replica", [(i, i ^ step) for i in range(replicas)])


def outer_finish(current, moment_now, total):
    drift_mean = total / lax.axis_size("replica")
    new_moment = outer_momentum * moment_now + drift_mean
    new_global = current - outer_rate * (drift_mean + outer_momentum * new_moment)
    return (new_global, new_moment)


def spot_of(chip, chips):
    back = jnp.where(chip == 0, 0, chips - lax.div(chip, 2))
    return jnp.where(lax.rem(chip, 2) == 1, lax.div(chip + 1, 2), back)


def chip_at(spot, chips):
    out = jnp.where(spot == 0, 0, 2 * spot - 1)
    return jnp.where(2 * spot <= chips, out, 2 * (chips - spot))


def inner_step(inputs, doc_ids, values, cotangent, weights, moment1, moment2, outer):
    devices = lax.axis_size("shard")
    chips = devices // 2
    here = lax.axis_index("shard")
    rows = weights.shape[0]
    part = rows // CHUNKS
    line = [0] + [i for i in range(chips) if i % 2 == 1] + [i for i in range(chips - 1, 1, -1) if i % 2 == 0]
    ring = [(2 * line[i] + c, 2 * line[(i + 1) % chips] + c) for i in range(chips) for c in range(2)]
    core = lax.rem(here, 2)
    spot = spot_of(lax.div(here, 2), chips)
    swap = [(i, i ^ 1) for i in range(devices)]

    def ordered(tokens, k):
        chip = chip_at(lax.rem(spot + (chips - k), chips), chips)
        return lax.dynamic_slice_in_dim(tokens, (2 * chip + core) * rows, rows, axis=1)

    blocks = [weights[j * part : (j + 1) * part].astype(jnp.bfloat16) for j in range(CHUNKS)]
    flying = [lax.ppermute(block, "shard", ring) for block in blocks]
    partner = lax.ppermute(inputs, "shard", swap)
    outer, flying[0] = lax.optimization_barrier((outer, flying[0]))
    current, moment_now, drift = outer_start(*outer)
    drift = exchange(drift, 1)
    both = [
        jnp.concatenate([ordered(inputs, k), ordered(partner, k)], axis=0) for k in range(chips)
    ]
    total = jnp.float32(0.0)
    for k in range(chips):
        for j in range(CHUNKS):
            total = total + jnp.dot(
                both[k][:, j * part : (j + 1) * part],
                blocks[j],
                preferred_element_type=jnp.float32,
            )
        if k < chips - 1:
            blocks = flying
            if k < chips - 2:
                flying = [lax.ppermute(block, "shard", ring) for block in blocks]
            if k == 0:
                drift, flying[0] = lax.optimization_barrier((drift, flying[0]))
                drift = exchange(drift, 2)
            if k == 1:
                drift, flying[0] = lax.optimization_barrier((drift, flying[0]))
                outer_done = outer_finish(current, moment_now, drift)
    tokens = inputs.shape[0]
    projected = total[:tokens] + lax.ppermute(total[tokens:], "shard", swap)
    grad_own = head_grads(inputs, doc_ids[0], values, cotangent, projected)
    grad_both = jnp.concatenate([grad_own, lax.ppermute(grad_own, "shard", swap)], axis=0)

    def term(k, j):
        return lax.dot_general(
            both[k][:, j * part : (j + 1) * part],
            grad_both,
            (((0,), (0,)), ((), ())),
            preferred_element_type=jnp.float32,
        )

    sums = [term(1, j).astype(jnp.bfloat16) for j in range(CHUNKS)]
    for k in range(chips - 1):
        later = 0 if k == chips - 2 else k + 2
        for j in range(CHUNKS):
            sums[j] = lax.ppermute(sums[j], "shard", ring).astype(jnp.float32) + term(later, j)
            if later:
                sums[j] = sums[j].astype(jnp.bfloat16)
    gradient = jnp.concatenate(sums, axis=0)
    first_new = beta_one * moment1 + (1.0 - beta_one) * gradient
    second_new = beta_two * moment2 + (1.0 - beta_two) * gradient * gradient
    first_hat = first_new / (1.0 - beta_one**ADAM_STEP)
    second_hat = second_new / (1.0 - beta_two**ADAM_STEP)
    weight_new = weights - learn_rate * (
        first_hat / (jnp.sqrt(second_hat) + 1e-08) + decay_rate * weights
    )
    return (weight_new, first_new, second_new) + outer_done


def on_device(
    inputs,
    doc_ids,
    values,
    cotangent,
    weights,
    moment1,
    moment2,
    frag_local,
    frag_global,
    frag_moment,
    frag_index,
):
    return inner_step(
        inputs,
        doc_ids,
        values,
        cotangent,
        weights,
        moment1,
        moment2,
        (frag_local, frag_global, frag_moment, frag_index),
    )


def solution(mesh):
    placed = (
        P(("replica", "shard"), None),
        P(("replica", "shard"), None),
        P(("replica", "shard"), None),
        P(("replica", "shard"), None),
        P(("replica", "shard"), None),
        P(("replica", "shard"), None),
        P(("replica", "shard"), None),
        P("replica", None, "shard", None),
        P(None, "shard", None),
        P(None, "shard", None),
        P(),
    )
    return jax.shard_map(
        on_device,
        mesh=mesh,
        in_specs=placed,
        out_specs=(
            P(("replica", "shard"), None),
            P(("replica", "shard"), None),
            P(("replica", "shard"), None),
            P("shard", None),
            P("shard", None),
        ),
        check_vma=False,
    )
```

```python
import math

import jax
import jax.numpy as jnp
from jax import lax
from jax.sharding import PartitionSpec as P

ADAM_STEP = 100
GATHER_CHUNKS = 3
SCATTER_CHUNKS = 3


epsilon = 1e-06
beta_one = 0.9
beta_two = 0.95
learn_rate = 0.01
decay_rate = 0.1
outer_momentum = 0.9
outer_rate = 0.7


def head_grads(inputs, doc_ids, values, cotangent, projected):
    model_width = inputs.shape[1]
    head_size = values.shape[1]
    input_scale = 1.0 / math.sqrt(model_width)
    score_scale = 1.0 / math.sqrt(head_size)
    scaled = projected * input_scale
    queries = scaled[:, :head_size]
    keys_part = scaled[:, head_size:]
    q_rate = lax.rsqrt(jnp.mean(queries * queries, axis=1, keepdims=True) + epsilon)
    k_rate = lax.rsqrt(jnp.mean(keys_part * keys_part, axis=1, keepdims=True) + epsilon)
    q_unit = queries * q_rate
    k_unit = keys_part * k_rate
    scores = jnp.dot(q_unit, k_unit.T, precision=lax.Precision.HIGH) * score_scale
    position = jnp.arange(doc_ids.shape[0])
    allowed = (doc_ids[:, None] == doc_ids[None, :]) & (position[None, :] <= position[:, None])
    raised = jnp.where(allowed, jnp.exp(scores), jnp.float32(0.0))
    attention = raised / jnp.sum(raised, axis=1, keepdims=True)
    grad_attention = jnp.dot(cotangent, values.T, preferred_element_type=jnp.float32)
    grad_scores = (
        attention
        * (grad_attention - jnp.sum(attention * grad_attention, axis=1, keepdims=True))
        * score_scale
    )
    grad_qunit = jnp.dot(grad_scores, k_unit, precision=lax.Precision.HIGH)
    grad_kunit = jnp.dot(grad_scores.T, q_unit, precision=lax.Precision.HIGH)
    grad_query = q_rate * (
        grad_qunit - q_unit * jnp.mean(grad_qunit * q_unit, axis=1, keepdims=True)
    )
    grad_keys = k_rate * (
        grad_kunit - k_unit * jnp.mean(grad_kunit * k_unit, axis=1, keepdims=True)
    )
    return (jnp.concatenate([grad_query, grad_keys], axis=1) * input_scale).astype(jnp.bfloat16)


def drift_of(outer):
    frag_local, frag_global, frag_moment, frag_index = outer
    chosen = frag_index[0]
    current = lax.dynamic_index_in_dim(frag_global, chosen, 0, keepdims=False)
    local_copy = lax.dynamic_index_in_dim(frag_local[0], chosen, 0, keepdims=False)
    drift = (current - local_copy.astype(jnp.float32)).astype(jnp.bfloat16)
    return lax.optimization_barrier(drift).astype(jnp.float32)


def exchange(total, step):
    replicas = lax.axis_size("replica")
    return total + lax.ppermute(total, "replica", [(i, i ^ step) for i in range(replicas)])


def outer_finish(outer, total):
    frag_local, frag_global, frag_moment, frag_index = outer
    chosen = frag_index[0]
    current = lax.dynamic_index_in_dim(frag_global, chosen, 0, keepdims=False)
    moment_now = lax.dynamic_index_in_dim(frag_moment, chosen, 0, keepdims=False)
    drift_mean = total / lax.axis_size("replica")
    new_moment = outer_momentum * moment_now + drift_mean
    new_global = current - outer_rate * (drift_mean + outer_momentum * new_moment)
    return (new_global, new_moment)


def adam(gradient, weights, moment1, moment2):
    first_new = beta_one * moment1 + (1.0 - beta_one) * gradient
    second_new = beta_two * moment2 + (1.0 - beta_two) * gradient * gradient
    first_hat = first_new / (1.0 - beta_one**ADAM_STEP)
    second_hat = second_new / (1.0 - beta_two**ADAM_STEP)
    weight_new = weights - learn_rate * (
        first_hat / (jnp.sqrt(second_hat) + 1e-08) + decay_rate * weights
    )
    return (weight_new, first_new, second_new)


def spot_of(chip, chips):
    back = jnp.where(chip == 0, 0, chips - lax.div(chip, 2))
    return jnp.where(lax.rem(chip, 2) == 1, lax.div(chip + 1, 2), back)


def chip_at(spot, chips):
    out = jnp.where(spot == 0, 0, 2 * spot - 1)
    return jnp.where(2 * spot <= chips, out, 2 * (chips - spot))


def inner_step(inputs, doc_ids, values, cotangent, weights, moment1, moment2, outer):
    devices = lax.axis_size("shard")
    chips = devices // 2
    here = lax.axis_index("shard")
    rows = weights.shape[0]
    line = [0] + [i for i in range(chips) if i % 2 == 1] + [i for i in range(chips - 1, 1, -1) if i % 2 == 0]
    ring = [(2 * line[i] + c, 2 * line[(i + 1) % chips] + c) for i in range(chips) for c in range(2)]
    core = lax.rem(here, 2)
    spot = spot_of(lax.div(here, 2), chips)
    swap = [(i, i ^ 1) for i in range(devices)]

    def ordered(tokens, k):
        chip = chip_at(lax.rem(spot + (chips - k), chips), chips)
        return lax.dynamic_slice_in_dim(tokens, (2 * chip + core) * rows, rows, axis=1)

    part = rows // GATHER_CHUNKS
    lowered = weights.astype(jnp.bfloat16)
    blocks = [lowered[j * part : (j + 1) * part] for j in range(GATHER_CHUNKS)]
    flying = [lax.ppermute(block, "shard", ring) for block in blocks]
    partner = lax.ppermute(inputs, "shard", swap)
    outer, flying[0] = lax.optimization_barrier((outer, flying[0]))
    drift = exchange(drift_of(outer), 1)
    both = [
        jnp.concatenate([ordered(inputs, k), ordered(partner, k)], axis=0) for k in range(chips)
    ]
    total = jnp.float32(0.0)
    for k in range(chips):
        if k in (0,):
            block = lowered if k == 0 else jnp.concatenate(blocks, axis=0)
            total = total + jnp.dot(both[k], block, preferred_element_type=jnp.float32)
        for j in range(GATHER_CHUNKS if k not in (0,) else 0):
            total = total + jnp.dot(
                both[k][:, j * part : (j + 1) * part],
                blocks[j],
                preferred_element_type=jnp.float32,
            )
        if k < chips - 1:
            blocks = flying
            if k < chips - 2:
                flying = [lax.ppermute(block, "shard", ring) for block in blocks]
            if k == 0:
                drift, flying[0] = lax.optimization_barrier((drift, flying[0]))
                drift = exchange(drift, 2)
            if k == 1:
                drift, flying[0] = lax.optimization_barrier((drift, flying[0]))
    tokens = inputs.shape[0]
    projected = total[:tokens] + lax.ppermute(total[tokens:], "shard", swap)
    grad_own = head_grads(inputs, doc_ids[0], values, cotangent, projected)
    grad_both = jnp.concatenate([grad_own, lax.ppermute(grad_own, "shard", swap)], axis=0)

    part = rows // SCATTER_CHUNKS

    def term(k, j):
        return lax.dot_general(
            both[k][:, j * part : (j + 1) * part],
            grad_both,
            (((0,), (0,)), ((), ())),
            preferred_element_type=jnp.float32,
        )

    sums = [term(1, j).astype(jnp.bfloat16) for j in range(SCATTER_CHUNKS)]
    for k in range(2, chips):
        for j in range(SCATTER_CHUNKS):
            came = lax.ppermute(sums[j], "shard", ring)
            sums[j] = (came.astype(jnp.float32) + term(k, j)).astype(jnp.bfloat16)
    for j in range(SCATTER_CHUNKS):
        sums[j] = lax.ppermute(sums[j], "shard", ring).astype(jnp.float32) + term(0, j)
    updated = adam(jnp.concatenate(sums, axis=0), weights, moment1, moment2)
    return updated + outer_finish(outer, drift)


def on_device(
    inputs,
    doc_ids,
    values,
    cotangent,
    weights,
    moment1,
    moment2,
    frag_local,
    frag_global,
    frag_moment,
    frag_index,
):
    return inner_step(
        inputs,
        doc_ids,
        values,
        cotangent,
        weights,
        moment1,
        moment2,
        (frag_local, frag_global, frag_moment, frag_index),
    )


def solution(mesh):
    placed = (
        P(("replica", "shard"), None),
        P(("replica", "shard"), None),
        P(("replica", "shard"), None),
        P(("replica", "shard"), None),
        P(("replica", "shard"), None),
        P(("replica", "shard"), None),
        P(("replica", "shard"), None),
        P("replica", None, "shard", None),
        P(None, "shard", None),
        P(None, "shard", None),
        P(),
    )
    return jax.shard_map(
        on_device,
        mesh=mesh,
        in_specs=placed,
        out_specs=(
            P(("replica", "shard"), None),
            P(("replica", "shard"), None),
            P(("replica", "shard"), None),
            P("shard", None),
            P("shard", None),
        ),
        check_vma=False,
    )
```

```python
import math

import jax
import jax.numpy as jnp
from jax import lax
from jax.sharding import PartitionSpec as P

ADAM_STEP = 100
GATHER_CHUNKS = 2
SCATTER_CHUNKS = 3


epsilon = 1e-06
beta_one = 0.9
beta_two = 0.95
learn_rate = 0.01
decay_rate = 0.1
outer_momentum = 0.9
outer_rate = 0.7


def head_grads(inputs, doc_ids, values, cotangent, projected):
    model_width = inputs.shape[1]
    head_size = values.shape[1]
    input_scale = 1.0 / math.sqrt(model_width)
    score_scale = 1.0 / math.sqrt(head_size)
    scaled = projected * input_scale
    queries = scaled[:, :head_size]
    keys_part = scaled[:, head_size:]
    q_rate = lax.rsqrt(jnp.mean(queries * queries, axis=1, keepdims=True) + epsilon)
    k_rate = lax.rsqrt(jnp.mean(keys_part * keys_part, axis=1, keepdims=True) + epsilon)
    q_unit = queries * q_rate
    k_unit = keys_part * k_rate
    scores = jnp.dot(q_unit, k_unit.T, precision=lax.Precision.HIGH) * score_scale
    position = jnp.arange(doc_ids.shape[0])
    allowed = (doc_ids[:, None] == doc_ids[None, :]) & (position[None, :] <= position[:, None])
    raised = jnp.where(allowed, jnp.exp(scores), jnp.float32(0.0))
    attention = raised / jnp.sum(raised, axis=1, keepdims=True)
    grad_attention = jnp.dot(cotangent, values.T, preferred_element_type=jnp.float32)
    grad_scores = (
        attention
        * (grad_attention - jnp.sum(attention * grad_attention, axis=1, keepdims=True))
        * score_scale
    )
    grad_qunit = jnp.dot(grad_scores, k_unit, precision=lax.Precision.HIGH)
    grad_kunit = jnp.dot(grad_scores.T, q_unit, precision=lax.Precision.HIGH)
    grad_query = q_rate * (
        grad_qunit - q_unit * jnp.mean(grad_qunit * q_unit, axis=1, keepdims=True)
    )
    grad_keys = k_rate * (
        grad_kunit - k_unit * jnp.mean(grad_kunit * k_unit, axis=1, keepdims=True)
    )
    return (jnp.concatenate([grad_query, grad_keys], axis=1) * input_scale).astype(jnp.bfloat16)


def outer_start(frag_local, frag_global, frag_moment, frag_index):
    chosen = frag_index[0]
    current = lax.dynamic_index_in_dim(frag_global, chosen, 0, keepdims=False)
    moment_now = lax.dynamic_index_in_dim(frag_moment, chosen, 0, keepdims=False)
    local_copy = lax.dynamic_index_in_dim(frag_local[0], chosen, 0, keepdims=False)
    drift = (current - local_copy.astype(jnp.float32)).astype(jnp.bfloat16)
    current, moment_now, drift = lax.optimization_barrier((current, moment_now, drift))
    return current, moment_now, drift.astype(jnp.float32)


def exchange(total, step):
    replicas = lax.axis_size("replica")
    return total + lax.ppermute(total, "replica", [(i, i ^ step) for i in range(replicas)])


def outer_finish(current, moment_now, total):
    drift_mean = total / lax.axis_size("replica")
    new_moment = outer_momentum * moment_now + drift_mean
    new_global = current - outer_rate * (drift_mean + outer_momentum * new_moment)
    return (new_global, new_moment)


def adam(gradient, weights, moment1, moment2):
    first_new = beta_one * moment1 + (1.0 - beta_one) * gradient
    second_new = beta_two * moment2 + (1.0 - beta_two) * gradient * gradient
    first_hat = first_new / (1.0 - beta_one**ADAM_STEP)
    second_hat = second_new / (1.0 - beta_two**ADAM_STEP)
    weight_new = weights - learn_rate * (
        first_hat / (jnp.sqrt(second_hat) + 1e-08) + decay_rate * weights
    )
    return (weight_new, first_new, second_new)


def spot_of(chip, chips):
    back = jnp.where(chip == 0, 0, chips - lax.div(chip, 2))
    return jnp.where(lax.rem(chip, 2) == 1, lax.div(chip + 1, 2), back)


def chip_at(spot, chips):
    out = jnp.where(spot == 0, 0, 2 * spot - 1)
    return jnp.where(2 * spot <= chips, out, 2 * (chips - spot))


def inner_step(inputs, doc_ids, values, cotangent, weights, moment1, moment2, outer):
    devices = lax.axis_size("shard")
    chips = devices // 2
    here = lax.axis_index("shard")
    rows = weights.shape[0]
    line = [0] + [i for i in range(chips) if i % 2 == 1] + [i for i in range(chips - 1, 1, -1) if i % 2 == 0]
    ring = [(2 * line[i] + c, 2 * line[(i + 1) % chips] + c) for i in range(chips) for c in range(2)]
    core = lax.rem(here, 2)
    spot = spot_of(lax.div(here, 2), chips)
    swap = [(i, i ^ 1) for i in range(devices)]

    def ordered(tokens, k):
        chip = chip_at(lax.rem(spot + (chips - k), chips), chips)
        return lax.dynamic_slice_in_dim(tokens, (2 * chip + core) * rows, rows, axis=1)

    part = rows // GATHER_CHUNKS
    lowered = weights.astype(jnp.bfloat16)
    blocks = [lowered[j * part : (j + 1) * part] for j in range(GATHER_CHUNKS)]
    flying = [lax.ppermute(block, "shard", ring) for block in blocks]
    partner = lax.ppermute(inputs, "shard", swap)
    current, moment_now, drift = outer_start(*outer)
    drift, flying[0] = lax.optimization_barrier((drift, flying[0]))
    drift = exchange(drift, 1)
    both = [
        jnp.concatenate([ordered(inputs, k), ordered(partner, k)], axis=0) for k in range(chips)
    ]
    total = jnp.float32(0.0)
    for k in range(chips):
        if k in (0,):
            block = lowered if k == 0 else jnp.concatenate(blocks, axis=0)
            total = total + jnp.dot(both[k], block, preferred_element_type=jnp.float32)
        for j in range(GATHER_CHUNKS if k not in (0,) else 0):
            total = total + jnp.dot(
                both[k][:, j * part : (j + 1) * part],
                blocks[j],
                preferred_element_type=jnp.float32,
            )
        if k < chips - 1:
            blocks = flying
            if k < chips - 2:
                flying = [lax.ppermute(block, "shard", ring) for block in blocks]
            if k == 0:
                drift, flying[0] = lax.optimization_barrier((drift, flying[0]))
                drift = exchange(drift, 2)
    tokens = inputs.shape[0]
    projected = total[:tokens] + lax.ppermute(total[tokens:], "shard", swap)
    grad_own = head_grads(inputs, doc_ids[0], values, cotangent, projected)
    grad_both = jnp.concatenate([grad_own, lax.ppermute(grad_own, "shard", swap)], axis=0)

    part = rows // SCATTER_CHUNKS

    def term(k, j):
        return lax.dot_general(
            both[k][:, j * part : (j + 1) * part],
            grad_both,
            (((0,), (0,)), ((), ())),
            preferred_element_type=jnp.float32,
        )

    sums = [term(1, j).astype(jnp.bfloat16) for j in range(SCATTER_CHUNKS)]
    for k in range(2, chips):
        for j in range(SCATTER_CHUNKS):
            came = lax.ppermute(sums[j], "shard", ring)
            sums[j] = (came.astype(jnp.float32) + term(k, j)).astype(jnp.bfloat16)
    for j in range(SCATTER_CHUNKS):
        sums[j] = lax.ppermute(sums[j], "shard", ring).astype(jnp.float32) + term(0, j)
    updated = adam(jnp.concatenate(sums, axis=0), weights, moment1, moment2)
    return updated + outer_finish(current, moment_now, drift)


def on_device(
    inputs,
    doc_ids,
    values,
    cotangent,
    weights,
    moment1,
    moment2,
    frag_local,
    frag_global,
    frag_moment,
    frag_index,
):
    return inner_step(
        inputs,
        doc_ids,
        values,
        cotangent,
        weights,
        moment1,
        moment2,
        (frag_local, frag_global, frag_moment, frag_index),
    )


def solution(mesh):
    placed = (
        P(("replica", "shard"), None),
        P(("replica", "shard"), None),
        P(("replica", "shard"), None),
        P(("replica", "shard"), None),
        P(("replica", "shard"), None),
        P(("replica", "shard"), None),
        P(("replica", "shard"), None),
        P("replica", None, "shard", None),
        P(None, "shard", None),
        P(None, "shard", None),
        P(),
    )
    return jax.shard_map(
        on_device,
        mesh=mesh,
        in_specs=placed,
        out_specs=(
            P(("replica", "shard"), None),
            P(("replica", "shard"), None),
            P(("replica", "shard"), None),
            P("shard", None),
            P("shard", None),
        ),
        check_vma=False,
    )
```

```python
import math

import jax
import jax.numpy as jnp
from jax import lax
from jax.sharding import PartitionSpec as P

ADAM_STEP = 100
GATHER_SHARES = (24, 24)
SCATTER_SHARES = (16, 16, 16)


epsilon = 1e-06
beta_one = 0.9
beta_two = 0.95
learn_rate = 0.01
decay_rate = 0.1
outer_momentum = 0.9
outer_rate = 0.7


def head_grads(inputs, doc_ids, values, cotangent, projected):
    model_width = inputs.shape[1]
    head_size = values.shape[1]
    input_scale = 1.0 / math.sqrt(model_width)
    score_scale = 1.0 / math.sqrt(head_size)
    scaled = projected * input_scale
    queries = scaled[:, :head_size]
    keys_part = scaled[:, head_size:]
    q_rate = lax.rsqrt(jnp.mean(queries * queries, axis=1, keepdims=True) + epsilon)
    k_rate = lax.rsqrt(jnp.mean(keys_part * keys_part, axis=1, keepdims=True) + epsilon)
    q_unit = queries * q_rate
    k_unit = keys_part * k_rate
    scores = jnp.dot(q_unit, k_unit.T, precision=lax.Precision.HIGH) * score_scale
    position = jnp.arange(doc_ids.shape[0])
    allowed = (doc_ids[:, None] == doc_ids[None, :]) & (position[None, :] <= position[:, None])
    raised = jnp.where(allowed, jnp.exp(scores), jnp.float32(0.0))
    attention = raised / jnp.sum(raised, axis=1, keepdims=True)
    grad_attention = jnp.dot(cotangent, values.T, preferred_element_type=jnp.float32)
    grad_scores = (
        attention
        * (grad_attention - jnp.sum(attention * grad_attention, axis=1, keepdims=True))
        * score_scale
    )
    grad_qunit = jnp.dot(grad_scores, k_unit, precision=lax.Precision.HIGH)
    grad_kunit = jnp.dot(grad_scores.T, q_unit, precision=lax.Precision.HIGH)
    grad_query = q_rate * (
        grad_qunit - q_unit * jnp.mean(grad_qunit * q_unit, axis=1, keepdims=True)
    )
    grad_keys = k_rate * (
        grad_kunit - k_unit * jnp.mean(grad_kunit * k_unit, axis=1, keepdims=True)
    )
    return (jnp.concatenate([grad_query, grad_keys], axis=1) * input_scale).astype(jnp.bfloat16)


def outer_start(frag_local, frag_global, frag_moment, frag_index):
    chosen = frag_index[0]
    current = lax.dynamic_index_in_dim(frag_global, chosen, 0, keepdims=False)
    moment_now = lax.dynamic_index_in_dim(frag_moment, chosen, 0, keepdims=False)
    local_copy = lax.dynamic_index_in_dim(frag_local[0], chosen, 0, keepdims=False)
    drift = (current - local_copy.astype(jnp.float32)).astype(jnp.bfloat16)
    current, moment_now, drift = lax.optimization_barrier((current, moment_now, drift))
    return current, moment_now, drift.astype(jnp.float32)


def exchange(total, step):
    replicas = lax.axis_size("replica")
    if step >= replicas:
        return total
    return total + lax.ppermute(total, "replica", [(i, i ^ step) for i in range(replicas)])


def outer_finish(current, moment_now, total):
    drift_mean = total / lax.axis_size("replica")
    new_moment = outer_momentum * moment_now + drift_mean
    new_global = current - outer_rate * (drift_mean + outer_momentum * new_moment)
    return (new_global, new_moment)


def adam(gradient, weights, moment1, moment2):
    first_new = beta_one * moment1 + (1.0 - beta_one) * gradient
    second_new = beta_two * moment2 + (1.0 - beta_two) * gradient * gradient
    first_hat = first_new / (1.0 - beta_one**ADAM_STEP)
    second_hat = second_new / (1.0 - beta_two**ADAM_STEP)
    weight_new = weights - learn_rate * (
        first_hat / (jnp.sqrt(second_hat) + 1e-08) + decay_rate * weights
    )
    return (weight_new, first_new, second_new)


def spans(rows, shares):
    ends = [rows * sum(shares[:j]) // sum(shares) for j in range(len(shares) + 1)]
    return [slice(a, b) for a, b in zip(ends[:-1], ends[1:])]


def spot_of(chip, chips):
    back = jnp.where(chip == 0, 0, chips - lax.div(chip, 2))
    return jnp.where(lax.rem(chip, 2) == 1, lax.div(chip + 1, 2), back)


def chip_at(spot, chips):
    out = jnp.where(spot == 0, 0, 2 * spot - 1)
    return jnp.where(2 * spot <= chips, out, 2 * (chips - spot))


def inner_step(inputs, doc_ids, values, cotangent, weights, moment1, moment2, outer):
    devices = lax.axis_size("shard")
    chips = devices // 2
    here = lax.axis_index("shard")
    rows = weights.shape[0]
    line = [0] + [i for i in range(chips) if i % 2 == 1] + [i for i in range(chips - 1, 1, -1) if i % 2 == 0]
    ring = [(2 * line[i] + c, 2 * line[(i + 1) % chips] + c) for i in range(chips) for c in range(2)]
    core = lax.rem(here, 2)
    spot = spot_of(lax.div(here, 2), chips)
    swap = [(i, i ^ 1) for i in range(devices)]

    def ordered(tokens, k):
        chip = chip_at(lax.rem(spot + (chips - k), chips), chips)
        return lax.dynamic_slice_in_dim(tokens, (2 * chip + core) * rows, rows, axis=1)

    cuts = spans(rows, GATHER_SHARES)
    lowered = weights.astype(jnp.bfloat16)
    blocks = [lowered[cut] for cut in cuts]
    flying = [lax.ppermute(block, "shard", ring) for block in blocks]
    partner = lax.ppermute(inputs, "shard", swap)
    current, moment_now, drift = outer_start(*outer)
    drift, flying[0] = lax.optimization_barrier((drift, flying[0]))
    drift = exchange(drift, 1)
    both = [
        jnp.concatenate([ordered(inputs, k), ordered(partner, k)], axis=0) for k in range(chips)
    ]
    for k in range(chips):
        if k == 0:
            total = jnp.dot(both[0], lowered, preferred_element_type=jnp.float32)
        else:
            for cut, block in zip(cuts, blocks):
                total = total + jnp.dot(
                    both[k][:, cut], block, preferred_element_type=jnp.float32
                )
        if k < chips - 1:
            blocks = flying
            if k < chips - 2:
                flying = [lax.ppermute(block, "shard", ring) for block in blocks]
            if k == 0:
                drift, flying[0] = lax.optimization_barrier((drift, flying[0]))
                step = 2
                while step < lax.axis_size("replica"):
                    drift = exchange(drift, step)
                    step = 2 * step
    tokens = inputs.shape[0]
    projected = total[:tokens] + lax.ppermute(total[tokens:], "shard", swap)
    grad_own = head_grads(inputs, doc_ids[0], values, cotangent, projected)
    grad_both = jnp.concatenate([grad_own, lax.ppermute(grad_own, "shard", swap)], axis=0)

    cuts = spans(rows, SCATTER_SHARES)

    def term(k, j):
        return lax.dot_general(
            both[k][:, cuts[j]],
            grad_both,
            (((0,), (0,)), ((), ())),
            preferred_element_type=jnp.float32,
        )

    sums = [term(1, j).astype(jnp.bfloat16) for j in range(len(cuts))]
    for k in range(2, chips):
        for j in range(len(cuts)):
            came = lax.ppermute(sums[j], "shard", ring)
            sums[j] = (came.astype(jnp.float32) + term(k, j)).astype(jnp.bfloat16)
    for j in range(len(cuts)):
        own = lax.optimization_barrier(term(0, j))
        sums[j] = lax.ppermute(sums[j], "shard", ring).astype(jnp.float32) + own
    updated = adam(jnp.concatenate(sums, axis=0), weights, moment1, moment2)
    return updated + outer_finish(current, moment_now, drift)


def on_device(
    inputs,
    doc_ids,
    values,
    cotangent,
    weights,
    moment1,
    moment2,
    frag_local,
    frag_global,
    frag_moment,
    frag_index,
):
    return inner_step(
        inputs,
        doc_ids,
        values,
        cotangent,
        weights,
        moment1,
        moment2,
        (frag_local, frag_global, frag_moment, frag_index),
    )


def solution(mesh):
    placed = (
        P(("replica", "shard"), None),
        P(("replica", "shard"), None),
        P(("replica", "shard"), None),
        P(("replica", "shard"), None),
        P(("replica", "shard"), None),
        P(("replica", "shard"), None),
        P(("replica", "shard"), None),
        P("replica", None, "shard", None),
        P(None, "shard", None),
        P(None, "shard", None),
        P(),
    )
    return jax.shard_map(
        on_device,
        mesh=mesh,
        in_specs=placed,
        out_specs=(
            P(("replica", "shard"), None),
            P(("replica", "shard"), None),
            P(("replica", "shard"), None),
            P("shard", None),
            P("shard", None),
        ),
        check_vma=False,
    )
```

```python
import math

import jax
import jax.numpy as jnp
from jax import lax
from jax.sharding import PartitionSpec as P

ADAM_STEP = 100
GATHER_SHARES = (24, 24)
SCATTER_SHARES = (16, 16, 16)


epsilon = 1e-06
beta_one = 0.9
beta_two = 0.95
learn_rate = 0.01
decay_rate = 0.1
outer_momentum = 0.9
outer_rate = 0.7


def head_grads(inputs, doc_ids, values, cotangent, projected):
    model_width = inputs.shape[1]
    head_size = values.shape[1]
    input_scale = 1.0 / math.sqrt(model_width)
    score_scale = 1.0 / math.sqrt(head_size)
    scaled = projected * input_scale
    queries = scaled[:, :head_size]
    keys_part = scaled[:, head_size:]
    q_rate = lax.rsqrt(jnp.mean(queries * queries, axis=1, keepdims=True) + epsilon)
    k_rate = lax.rsqrt(jnp.mean(keys_part * keys_part, axis=1, keepdims=True) + epsilon)
    q_unit = queries * q_rate
    k_unit = keys_part * k_rate
    scores = jnp.dot(q_unit, k_unit.T, precision=lax.Precision.HIGH) * score_scale
    position = jnp.arange(doc_ids.shape[0])
    allowed = (doc_ids[:, None] == doc_ids[None, :]) & (position[None, :] <= position[:, None])
    raised = jnp.where(allowed, jnp.exp(scores), jnp.float32(0.0))
    attention = raised / jnp.sum(raised, axis=1, keepdims=True)
    grad_attention = jnp.dot(cotangent, values.T, preferred_element_type=jnp.float32)
    grad_scores = (
        attention
        * (grad_attention - jnp.sum(attention * grad_attention, axis=1, keepdims=True))
        * score_scale
    )
    grad_qunit = jnp.dot(grad_scores, k_unit, precision=lax.Precision.HIGH)
    grad_kunit = jnp.dot(grad_scores.T, q_unit, precision=lax.Precision.HIGH)
    grad_query = q_rate * (
        grad_qunit - q_unit * jnp.mean(grad_qunit * q_unit, axis=1, keepdims=True)
    )
    grad_keys = k_rate * (
        grad_kunit - k_unit * jnp.mean(grad_kunit * k_unit, axis=1, keepdims=True)
    )
    return (jnp.concatenate([grad_query, grad_keys], axis=1) * input_scale).astype(jnp.bfloat16)


def outer_start(frag_local, frag_global, frag_moment, frag_index):
    chosen = frag_index[0]
    current = lax.dynamic_index_in_dim(frag_global, chosen, 0, keepdims=False)
    moment_now = lax.dynamic_index_in_dim(frag_moment, chosen, 0, keepdims=False)
    local_copy = lax.dynamic_index_in_dim(frag_local[0], chosen, 0, keepdims=False)
    drift = (current - local_copy.astype(jnp.float32)).astype(jnp.bfloat16)
    current, moment_now, drift = lax.optimization_barrier((current, moment_now, drift))
    return current, moment_now, drift.astype(jnp.float32)


def exchange(total, step):
    replicas = lax.axis_size("replica")
    if step >= replicas:
        return total
    return total + lax.ppermute(total, "replica", [(i, i ^ step) for i in range(replicas)])


def outer_finish(current, moment_now, total):
    drift_mean = total / lax.axis_size("replica")
    new_moment = outer_momentum * moment_now + drift_mean
    new_global = current - outer_rate * (drift_mean + outer_momentum * new_moment)
    return (new_global, new_moment)


def adam(gradient, weights, moment1, moment2):
    first_new = beta_one * moment1 + (1.0 - beta_one) * gradient
    second_new = beta_two * moment2 + (1.0 - beta_two) * gradient * gradient
    first_hat = first_new / (1.0 - beta_one**ADAM_STEP)
    second_hat = second_new / (1.0 - beta_two**ADAM_STEP)
    weight_new = weights - learn_rate * (
        first_hat / (jnp.sqrt(second_hat) + 1e-08) + decay_rate * weights
    )
    return (weight_new, first_new, second_new)


def spans(rows, shares):
    ends = [rows * sum(shares[:j]) // sum(shares) for j in range(len(shares) + 1)]
    return [slice(a, b) for a, b in zip(ends[:-1], ends[1:])]


def spot_of(chip, chips):
    back = chips - lax.div(chip + 1, 2)
    return jnp.where(lax.rem(chip, 2) == 0, lax.div(chip, 2), back)


def chip_at(spot, chips):
    return jnp.where(2 * spot < chips, 2 * spot, 2 * (chips - spot) - 1)


def inner_step(inputs, doc_ids, values, cotangent, weights, moment1, moment2, outer):
    devices = lax.axis_size("shard")
    chips = devices // 2
    here = lax.axis_index("shard")
    rows = weights.shape[0]
    line = list(range(0, chips, 2)) + list(range(chips - 1 - chips % 2, 0, -2))
    ring = [(2 * line[i] + c, 2 * line[(i + 1) % chips] + c) for i in range(chips) for c in range(2)]
    core = lax.rem(here, 2)
    spot = spot_of(lax.div(here, 2), chips)
    swap = [(i, i ^ 1) for i in range(devices)]

    def ordered(tokens, k):
        chip = chip_at(lax.rem(spot + (chips - k), chips), chips)
        return lax.dynamic_slice_in_dim(tokens, (2 * chip + core) * rows, rows, axis=1)

    cuts = spans(rows, GATHER_SHARES)
    lowered = weights.astype(jnp.bfloat16)
    blocks = [lowered[cut] for cut in cuts]
    flying = [lax.ppermute(block, "shard", ring) for block in blocks]
    partner = lax.ppermute(inputs, "shard", swap)
    current, moment_now, drift = outer_start(*outer)
    drift, flying[0] = lax.optimization_barrier((drift, flying[0]))
    drift = exchange(drift, 1)
    both = [
        jnp.concatenate([ordered(inputs, k), ordered(partner, k)], axis=0) for k in range(chips)
    ]
    for k in range(chips):
        if k == 0:
            total = jnp.dot(both[0], lowered, preferred_element_type=jnp.float32)
        else:
            for cut, block in zip(cuts, blocks):
                total = total + jnp.dot(
                    both[k][:, cut], block, preferred_element_type=jnp.float32
                )
        if k < chips - 1:
            blocks = flying
            if k < chips - 2:
                flying = [lax.ppermute(block, "shard", ring) for block in blocks]
            if k == 0:
                drift, flying[0] = lax.optimization_barrier((drift, flying[0]))
                step = 2
                while step < lax.axis_size("replica"):
                    drift = exchange(drift, step)
                    step = 2 * step
    tokens = inputs.shape[0]
    projected = total[:tokens] + lax.ppermute(total[tokens:], "shard", swap)
    grad_own = head_grads(inputs, doc_ids[0], values, cotangent, projected)
    grad_both = jnp.concatenate([grad_own, lax.ppermute(grad_own, "shard", swap)], axis=0)

    cuts = spans(rows, SCATTER_SHARES)

    def term(k, j):
        return lax.dot_general(
            both[k][:, cuts[j]],
            grad_both,
            (((0,), (0,)), ((), ())),
            preferred_element_type=jnp.float32,
        )

    sums = [term(1, j).astype(jnp.bfloat16) for j in range(len(cuts))]
    for k in range(2, chips):
        for j in range(len(cuts)):
            came = lax.ppermute(sums[j], "shard", ring)
            sums[j] = (came.astype(jnp.float32) + term(k, j)).astype(jnp.bfloat16)
    for j in range(len(cuts)):
        own = lax.optimization_barrier(term(0, j))
        sums[j] = lax.ppermute(sums[j], "shard", ring).astype(jnp.float32) + own
    updated = adam(jnp.concatenate(sums, axis=0), weights, moment1, moment2)
    return updated + outer_finish(current, moment_now, drift)


def on_device(
    inputs,
    doc_ids,
    values,
    cotangent,
    weights,
    moment1,
    moment2,
    frag_local,
    frag_global,
    frag_moment,
    frag_index,
):
    return inner_step(
        inputs,
        doc_ids,
        values,
        cotangent,
        weights,
        moment1,
        moment2,
        (frag_local, frag_global, frag_moment, frag_index),
    )


def solution(mesh):
    placed = (
        P(("replica", "shard"), None),
        P(("replica", "shard"), None),
        P(("replica", "shard"), None),
        P(("replica", "shard"), None),
        P(("replica", "shard"), None),
        P(("replica", "shard"), None),
        P(("replica", "shard"), None),
        P("replica", None, "shard", None),
        P(None, "shard", None),
        P(None, "shard", None),
        P(),
    )
    return jax.shard_map(
        on_device,
        mesh=mesh,
        in_specs=placed,
        out_specs=(
            P(("replica", "shard"), None),
            P(("replica", "shard"), None),
            P(("replica", "shard"), None),
            P("shard", None),
            P("shard", None),
        ),
        check_vma=False,
    )
```

```python
import math

import jax
import jax.numpy as jnp
from jax import lax
from jax.sharding import PartitionSpec as P

ADAM_STEP = 100
GATHER_SHARES = (24, 24)
SCATTER_SHARES = (16, 16, 16)


epsilon = 1e-06
beta_one = 0.9
beta_two = 0.95
learn_rate = 0.01
decay_rate = 0.1
outer_momentum = 0.9
outer_rate = 0.7


def head_grads(inputs, doc_ids, values, cotangent, projected):
    model_width = inputs.shape[1]
    head_size = values.shape[1]
    input_scale = 1.0 / math.sqrt(model_width)
    score_scale = 1.0 / math.sqrt(head_size)
    scaled = projected * input_scale
    queries = scaled[:, :head_size]
    keys_part = scaled[:, head_size:]
    q_rate = lax.rsqrt(jnp.mean(queries * queries, axis=1, keepdims=True) + epsilon)
    k_rate = lax.rsqrt(jnp.mean(keys_part * keys_part, axis=1, keepdims=True) + epsilon)
    q_unit = queries * q_rate
    k_unit = keys_part * k_rate
    scores = jnp.dot(q_unit, k_unit.T, precision=lax.Precision.HIGH) * score_scale
    position = jnp.arange(doc_ids.shape[0])
    allowed = (doc_ids[:, None] == doc_ids[None, :]) & (position[None, :] <= position[:, None])
    raised = jnp.where(allowed, jnp.exp(scores), jnp.float32(0.0))
    attention = raised / jnp.sum(raised, axis=1, keepdims=True)
    grad_attention = jnp.dot(cotangent, values.T, preferred_element_type=jnp.float32)
    grad_scores = (
        attention
        * (grad_attention - jnp.sum(attention * grad_attention, axis=1, keepdims=True))
        * score_scale
    )
    grad_qunit = jnp.dot(grad_scores, k_unit, precision=lax.Precision.HIGH)
    grad_kunit = jnp.dot(grad_scores.T, q_unit, precision=lax.Precision.HIGH)
    grad_query = q_rate * (
        grad_qunit - q_unit * jnp.mean(grad_qunit * q_unit, axis=1, keepdims=True)
    )
    grad_keys = k_rate * (
        grad_kunit - k_unit * jnp.mean(grad_kunit * k_unit, axis=1, keepdims=True)
    )
    return (jnp.concatenate([grad_query, grad_keys], axis=1) * input_scale).astype(jnp.bfloat16)


def outer_start(frag_local, frag_global, frag_moment, frag_index):
    chosen = frag_index[0]
    current = lax.dynamic_index_in_dim(frag_global, chosen, 0, keepdims=False)
    moment_now = lax.dynamic_index_in_dim(frag_moment, chosen, 0, keepdims=False)
    local_copy = lax.dynamic_index_in_dim(frag_local[0], chosen, 0, keepdims=False)
    drift = (current - local_copy.astype(jnp.float32)).astype(jnp.bfloat16)
    current, moment_now, drift = lax.optimization_barrier((current, moment_now, drift))
    return current, moment_now, drift.astype(jnp.float32)


def exchange(total, step):
    replicas = lax.axis_size("replica")
    if step >= replicas:
        return total
    return total + lax.ppermute(total, "replica", [(i, i ^ step) for i in range(replicas)])


def outer_finish(current, moment_now, total):
    drift_mean = total / lax.axis_size("replica")
    new_moment = outer_momentum * moment_now + drift_mean
    new_global = current - outer_rate * (drift_mean + outer_momentum * new_moment)
    return (new_global, new_moment)


def adam(gradient, weights, moment1, moment2):
    first_new = beta_one * moment1 + (1.0 - beta_one) * gradient
    second_new = beta_two * moment2 + (1.0 - beta_two) * gradient * gradient
    first_hat = first_new / (1.0 - beta_one**ADAM_STEP)
    second_hat = second_new / (1.0 - beta_two**ADAM_STEP)
    weight_new = weights - learn_rate * (
        first_hat / (jnp.sqrt(second_hat) + 1e-08) + decay_rate * weights
    )
    return (weight_new, first_new, second_new)


def spans(rows, shares):
    ends = [rows * sum(shares[:j]) // sum(shares) for j in range(len(shares) + 1)]
    return [slice(a, b) for a, b in zip(ends[:-1], ends[1:])]


def spot_of(chip, chips):
    back = chips - lax.div(chip + 1, 2)
    return jnp.where(lax.rem(chip, 2) == 0, lax.div(chip, 2), back)


def chip_at(spot, chips):
    return jnp.where(2 * spot < chips, 2 * spot, 2 * (chips - spot) - 1)


def inner_step(inputs, doc_ids, values, cotangent, weights, moment1, moment2, outer):
    devices = lax.axis_size("shard")
    chips = devices // 2
    here = lax.axis_index("shard")
    rows = weights.shape[0]
    line = list(range(0, chips, 2)) + list(range(chips - 1 - chips % 2, 0, -2))
    ring = [(2 * line[i] + c, 2 * line[(i + 1) % chips] + c) for i in range(chips) for c in range(2)]
    core = lax.rem(here, 2)
    spot = spot_of(lax.div(here, 2), chips)
    swap = [(i, i ^ 1) for i in range(devices)]

    def ordered(tokens, k):
        chip = chip_at(lax.rem(spot + (chips - k), chips), chips)
        return lax.dynamic_slice_in_dim(tokens, (2 * chip + core) * rows, rows, axis=1)

    cuts = spans(rows, GATHER_SHARES)
    lowered = weights.astype(jnp.bfloat16)
    blocks = [lowered[cut] for cut in cuts]
    flying = [lax.ppermute(block, "shard", ring) for block in blocks]
    partner = lax.ppermute(inputs, "shard", swap)
    current, moment_now, drift = outer_start(*outer)
    drift, flying[-1] = lax.optimization_barrier((drift, flying[-1]))
    drift = exchange(drift, 1)
    both = [
        jnp.concatenate([ordered(inputs, k), ordered(partner, k)], axis=0) for k in range(chips)
    ]
    for k in range(chips):
        if k == 0:
            total = jnp.dot(both[0], lowered, preferred_element_type=jnp.float32)
        else:
            for cut, block in zip(cuts, blocks):
                total = total + jnp.dot(
                    both[k][:, cut], block, preferred_element_type=jnp.float32
                )
        if k < chips - 1:
            blocks = flying
            if k < chips - 2:
                flying = [lax.ppermute(block, "shard", ring) for block in blocks]
            if k == 0:
                drift, flying[-1] = lax.optimization_barrier((drift, flying[-1]))
                step = 2
                while step < lax.axis_size("replica"):
                    drift = exchange(drift, step)
                    step = 2 * step
    tokens = inputs.shape[0]
    projected = total[:tokens] + lax.ppermute(total[tokens:], "shard", swap)
    grad_own = head_grads(inputs, doc_ids[0], values, cotangent, projected)
    grad_both = jnp.concatenate([grad_own, lax.ppermute(grad_own, "shard", swap)], axis=0)

    cuts = spans(rows, SCATTER_SHARES)

    def term(k, j):
        return lax.dot_general(
            both[k][:, cuts[j]],
            grad_both,
            (((0,), (0,)), ((), ())),
            preferred_element_type=jnp.float32,
        )

    sums = [term(1, j).astype(jnp.bfloat16) for j in range(len(cuts))]
    for k in range(2, chips):
        for j in range(len(cuts)):
            came = lax.ppermute(sums[j], "shard", ring)
            sums[j] = (came.astype(jnp.float32) + term(k, j)).astype(jnp.bfloat16)
    for j in range(len(cuts)):
        own = lax.optimization_barrier(term(0, j))
        sums[j] = lax.ppermute(sums[j], "shard", ring).astype(jnp.float32) + own
    updated = adam(jnp.concatenate(sums, axis=0), weights, moment1, moment2)
    return updated + outer_finish(current, moment_now, drift)


def on_device(
    inputs,
    doc_ids,
    values,
    cotangent,
    weights,
    moment1,
    moment2,
    frag_local,
    frag_global,
    frag_moment,
    frag_index,
):
    return inner_step(
        inputs,
        doc_ids,
        values,
        cotangent,
        weights,
        moment1,
        moment2,
        (frag_local, frag_global, frag_moment, frag_index),
    )


def solution(mesh):
    placed = (
        P(("replica", "shard"), None),
        P(("replica", "shard"), None),
        P(("replica", "shard"), None),
        P(("replica", "shard"), None),
        P(("replica", "shard"), None),
        P(("replica", "shard"), None),
        P(("replica", "shard"), None),
        P("replica", None, "shard", None),
        P(None, "shard", None),
        P(None, "shard", None),
        P(),
    )
    return jax.shard_map(
        on_device,
        mesh=mesh,
        in_specs=placed,
        out_specs=(
            P(("replica", "shard"), None),
            P(("replica", "shard"), None),
            P(("replica", "shard"), None),
            P("shard", None),
            P("shard", None),
        ),
        check_vma=False,
    )
```

```python
import math

import jax
import jax.numpy as jnp
from jax import lax
from jax.sharding import PartitionSpec as P

ADAM_STEP = 100
GATHER_SHARES = (16, 16, 16)
SCATTER_SHARES = (16, 16, 16)


epsilon = 1e-06
beta_one = 0.9
beta_two = 0.95
learn_rate = 0.01
decay_rate = 0.1
outer_momentum = 0.9
outer_rate = 0.7


def head_grads(inputs, doc_ids, values, cotangent, projected):
    model_width = inputs.shape[1]
    head_size = values.shape[1]
    input_scale = 1.0 / math.sqrt(model_width)
    score_scale = 1.0 / math.sqrt(head_size)
    scaled = projected * input_scale
    queries = scaled[:, :head_size]
    keys_part = scaled[:, head_size:]
    q_rate = lax.rsqrt(jnp.mean(queries * queries, axis=1, keepdims=True) + epsilon)
    k_rate = lax.rsqrt(jnp.mean(keys_part * keys_part, axis=1, keepdims=True) + epsilon)
    q_unit = queries * q_rate
    k_unit = keys_part * k_rate
    scores = jnp.dot(q_unit, k_unit.T, precision=lax.Precision.HIGH) * score_scale
    position = jnp.arange(doc_ids.shape[0])
    allowed = (doc_ids[:, None] == doc_ids[None, :]) & (position[None, :] <= position[:, None])
    raised = jnp.where(allowed, jnp.exp(scores), jnp.float32(0.0))
    attention = raised / jnp.sum(raised, axis=1, keepdims=True)
    grad_attention = jnp.dot(cotangent, values.T, preferred_element_type=jnp.float32)
    grad_scores = (
        attention
        * (grad_attention - jnp.sum(attention * grad_attention, axis=1, keepdims=True))
        * score_scale
    )
    grad_qunit = jnp.dot(grad_scores, k_unit, precision=lax.Precision.HIGH)
    grad_kunit = jnp.dot(grad_scores.T, q_unit, precision=lax.Precision.HIGH)
    grad_query = q_rate * (
        grad_qunit - q_unit * jnp.mean(grad_qunit * q_unit, axis=1, keepdims=True)
    )
    grad_keys = k_rate * (
        grad_kunit - k_unit * jnp.mean(grad_kunit * k_unit, axis=1, keepdims=True)
    )
    return (jnp.concatenate([grad_query, grad_keys], axis=1) * input_scale).astype(jnp.bfloat16)


def outer_start(frag_local, frag_global, frag_moment, frag_index):
    chosen = frag_index[0]
    current = lax.dynamic_index_in_dim(frag_global, chosen, 0, keepdims=False)
    moment_now = lax.dynamic_index_in_dim(frag_moment, chosen, 0, keepdims=False)
    local_copy = lax.dynamic_index_in_dim(frag_local[0], chosen, 0, keepdims=False)
    drift = (current - local_copy.astype(jnp.float32)).astype(jnp.bfloat16)
    current, moment_now, drift = lax.optimization_barrier((current, moment_now, drift))
    return current, moment_now, drift.astype(jnp.float32)


def exchange(total, step):
    replicas = lax.axis_size("replica")
    if step >= replicas:
        return total
    return total + lax.ppermute(total, "replica", [(i, i ^ step) for i in range(replicas)])


def outer_finish(current, moment_now, total):
    drift_mean = total / lax.axis_size("replica")
    new_moment = outer_momentum * moment_now + drift_mean
    new_global = current - outer_rate * (drift_mean + outer_momentum * new_moment)
    return (new_global, new_moment)


def adam(gradient, weights, moment1, moment2):
    first_new = beta_one * moment1 + (1.0 - beta_one) * gradient
    second_new = beta_two * moment2 + (1.0 - beta_two) * gradient * gradient
    first_hat = first_new / (1.0 - beta_one**ADAM_STEP)
    second_hat = second_new / (1.0 - beta_two**ADAM_STEP)
    weight_new = weights - learn_rate * (
        first_hat / (jnp.sqrt(second_hat) + 1e-08) + decay_rate * weights
    )
    return (weight_new, first_new, second_new)


def spans(rows, shares):
    ends = [rows * sum(shares[:j]) // sum(shares) for j in range(len(shares) + 1)]
    return [slice(a, b) for a, b in zip(ends[:-1], ends[1:])]


def spot_of(chip, chips):
    back = chips - lax.div(chip + 1, 2)
    return jnp.where(lax.rem(chip, 2) == 0, lax.div(chip, 2), back)


def chip_at(spot, chips):
    return jnp.where(2 * spot < chips, 2 * spot, 2 * (chips - spot) - 1)


def inner_step(inputs, doc_ids, values, cotangent, weights, moment1, moment2, outer):
    devices = lax.axis_size("shard")
    chips = devices // 2
    here = lax.axis_index("shard")
    rows = weights.shape[0]
    line = list(range(0, chips, 2)) + list(range(chips - 1 - chips % 2, 0, -2))
    ring = [(2 * line[i] + c, 2 * line[(i + 1) % chips] + c) for i in range(chips) for c in range(2)]
    core = lax.rem(here, 2)
    spot = spot_of(lax.div(here, 2), chips)
    swap = [(i, i ^ 1) for i in range(devices)]

    def ordered(tokens, k):
        chip = chip_at(lax.rem(spot + (chips - k), chips), chips)
        return lax.dynamic_slice_in_dim(tokens, (2 * chip + core) * rows, rows, axis=1)

    cuts = spans(rows, GATHER_SHARES)
    lowered = weights.astype(jnp.bfloat16)
    blocks = [lowered[cut] for cut in cuts]
    flying = [lax.ppermute(block, "shard", ring) for block in blocks]
    partner = lax.ppermute(inputs, "shard", swap)
    current, moment_now, drift = outer_start(*outer)
    drift, flying[0] = lax.optimization_barrier((drift, flying[0]))
    drift = exchange(drift, 1)
    both = [
        jnp.concatenate([ordered(inputs, k), ordered(partner, k)], axis=0) for k in range(chips)
    ]
    for k in range(chips):
        if k == 0:
            total = jnp.dot(both[0], lowered, preferred_element_type=jnp.float32)
        else:
            for cut, block in zip(cuts, blocks):
                total = total + jnp.dot(
                    both[k][:, cut], block, preferred_element_type=jnp.float32
                )
        if k < chips - 1:
            blocks = flying
            if k < chips - 2:
                flying = [lax.ppermute(block, "shard", ring) for block in blocks]
            if k == 0:
                drift, flying[0] = lax.optimization_barrier((drift, flying[0]))
                step = 2
                while step < lax.axis_size("replica"):
                    drift = exchange(drift, step)
                    step = 2 * step
    tokens = inputs.shape[0]
    projected = total[:tokens] + lax.ppermute(total[tokens:], "shard", swap)
    grad_own = head_grads(inputs, doc_ids[0], values, cotangent, projected)
    grad_both = jnp.concatenate([grad_own, lax.ppermute(grad_own, "shard", swap)], axis=0)

    cuts = spans(rows, SCATTER_SHARES)

    def term(k, j):
        return lax.dot_general(
            both[k][:, cuts[j]],
            grad_both,
            (((0,), (0,)), ((), ())),
            preferred_element_type=jnp.float32,
        )

    sums = [term(1, j).astype(jnp.bfloat16) for j in range(len(cuts))]
    for k in range(2, chips):
        for j in range(len(cuts)):
            came = lax.ppermute(sums[j], "shard", ring)
            sums[j] = (came.astype(jnp.float32) + term(k, j)).astype(jnp.bfloat16)
    for j in range(len(cuts)):
        own = lax.optimization_barrier(term(0, j))
        sums[j] = lax.ppermute(sums[j], "shard", ring).astype(jnp.float32) + own
    updated = adam(jnp.concatenate(sums, axis=0), weights, moment1, moment2)
    return updated + outer_finish(current, moment_now, drift)


def on_device(
    inputs,
    doc_ids,
    values,
    cotangent,
    weights,
    moment1,
    moment2,
    frag_local,
    frag_global,
    frag_moment,
    frag_index,
):
    return inner_step(
        inputs,
        doc_ids,
        values,
        cotangent,
        weights,
        moment1,
        moment2,
        (frag_local, frag_global, frag_moment, frag_index),
    )


def solution(mesh):
    placed = (
        P(("replica", "shard"), None),
        P(("replica", "shard"), None),
        P(("replica", "shard"), None),
        P(("replica", "shard"), None),
        P(("replica", "shard"), None),
        P(("replica", "shard"), None),
        P(("replica", "shard"), None),
        P("replica", None, "shard", None),
        P(None, "shard", None),
        P(None, "shard", None),
        P(),
    )
    return jax.shard_map(
        on_device,
        mesh=mesh,
        in_specs=placed,
        out_specs=(
            P(("replica", "shard"), None),
            P(("replica", "shard"), None),
            P(("replica", "shard"), None),
            P("shard", None),
            P("shard", None),
        ),
        check_vma=False,
    )
```
